256 devices in a mesh: pts: 128 (over y, x, z), rep: 2 (over core).
Axes of the slice: x: 4, y: 4, z: 8, core: 2. Of those that a mesh axis runs over, the one named last changes fastest.
Arguments:
- features: bfloat16 [262144, 256], P(('rep', 'pts')), parts along dimension 0, may hold values from -6 to 6
- hilbert_rank: int32 [262144], P(('rep', 'pts')), parts along dimension 0, may hold values from 0 to 131071, as said below
- point_mask: int32 [262144], P(('rep', 'pts')), parts along dimension 0, may hold values 0 or 1
- norm_gains: bfloat16 [5, 256], replicated, may hold values from 0.5 to 1.5
- w_qkv: bfloat16 [2, 256, 768], replicated
- w_out: bfloat16 [2, 256, 256], replicated, may hold values from -0.375 to 0.375
- w_up: bfloat16 [2, 256, 1024], replicated, may hold values from -0.375 to 0.375
- w_down: bfloat16 [2, 1024, 256], replicated, may hold values from -0.1875 to 0.1875
- head_hidden: bfloat16 [256, 256], replicated, may hold values from -0.375 to 0.375
- head_out: bfloat16 [256, 4], replicated, may hold values from -0.375 to 0.375
Outputs:
- offsets: float32 [262144, 4], P(('rep', 'pts')), parts along dimension 0
The draws below stay inside these ranges and needn't reach their ends.
There are 2 independent parts, one for each index of `rep`. The reference program is written for one: setup_inputs(seed, part) draws one part's arguments, and reference() takes and returns one part's arrays. A program takes and returns all parts, laid end to end along the dimension named above; an argument that names none is the same for every part. Nothing has to cross between parts.
Inputs may be any that keep to these rules, and one draw needn't show every extreme that they name: `hilbert_rank`: A permutation of the points. Of the 1024 points of one device, at most 16 have ranks in any one block of 1024 ranks; some device sends exactly 16 to some block in every draw.
All inputs are finite; a program needn't handle non-finite values. No bound on the sum of `point_mask` on one device may be relied on, other than what follows from the above.
Results may differ from the reference program's by a relative error of at most 0.033.
The reference program's roundings to bfloat16 on the way count: a program that leaves them out, or rounds other values in their place, can miss the bound.
Values may be sent and summed in bfloat16 or wider, within the bound.
A program may use at most 64 MiB of HBM per device.

```python
import jax
import jax.numpy as jnp
from jax import lax

D = 256
HEADS = 16
FF = 1024
PATCH = 1024
OUTS = 4
POINTS_PER_SHARD = 1024
POINTS = 131072
N_PTS = 128


def draw_w_qkv(key, part):
    key = jax.random.fold_in(key, 1)
    base = jax.random.normal(key, (2, D, 3 * D), jnp.float32) * D ** (-0.5)
    return base.astype(jnp.bfloat16)


def draw_hilbert_rank(key, part):
    key = jax.random.fold_in(key, 11)
    random_keys = jax.random.split(key, 5)
    mean = POINTS_PER_SHARD // N_PTS
    places = jnp.arange(N_PTS, dtype=jnp.int32)
    lift = jax.random.randint(random_keys[0], (N_PTS,), 0, mean + 1).astype(jnp.int32)
    peak = jax.random.randint(random_keys[1], (), 0, N_PTS).astype(jnp.int32)
    lift = jnp.where(places == peak, mean, lift)
    lift = jnp.where(places == (peak + 1) % N_PTS, 0, lift)
    share = mean + lift - jnp.roll(lift, -1)
    relabel = jax.random.permutation(random_keys[2], N_PTS).astype(jnp.int32)
    counts = share[(relabel[None, :] - relabel[:, None]) % N_PTS]
    ends = jnp.cumsum(counts, axis=1)
    starts = jnp.cumsum(counts, axis=0) - counts
    inside = jnp.arange(POINTS_PER_SHARD, dtype=jnp.int32)

    def single_sender(sender_shard, sample_key):
        point_permute = jax.random.permutation(sample_key, POINTS_PER_SHARD).astype(jnp.int32)
        target = jnp.searchsorted(ends[sender_shard], inside, side='right').astype(jnp.int32)
        within = inside - (ends[sender_shard][target] - counts[sender_shard][target])
        return (point_permute, target, starts[sender_shard][target] + within)
    shuffles, targets, spots = jax.vmap(single_sender)(places, jax.random.split(random_keys[3], N_PTS))
    slot_orderings = jax.vmap(lambda sample_key: jax.random.permutation(sample_key, POINTS_PER_SHARD).astype(jnp.int32))(jax.random.split(random_keys[4], N_PTS))
    ranks = targets * POINTS_PER_SHARD + slot_orderings[targets, spots]
    owners = places[:, None] * POINTS_PER_SHARD + shuffles
    return jnp.zeros((POINTS,), jnp.int32).at[owners.reshape(-1)].set(ranks.reshape(-1))


def set_ends(values, key, least, largest):
    index_at = [jax.random.randint(jax.random.fold_in(key, axis), (), 0, length) for axis, length in enumerate(values.shape)]
    widest = values.shape.index(max(values.shape))
    next_to = index_at[:widest] + [(index_at[widest] + 1) % values.shape[widest]] + index_at[widest + 1:]
    return values.at[tuple(index_at)].set(least).at[tuple(next_to)].set(largest)


def levels(own_key, dims, shards, least, high):
    level, own = 1.0, jax.random.fold_in(own_key, 6)
    for position, shards_of in shards:
        steps = jnp.exp(jax.random.uniform(jax.random.fold_in(own, position), (shards_of,), jnp.float32, least / len(shards), high / len(shards)))
        level = level * jnp.repeat(steps, dims[position] // shards_of).reshape([-1 if axis == position else 1 for axis in range(len(dims))])
    return level


def normal_values(stream_key, dims, deviation, reach, cuts=(), kind=jnp.bfloat16):
    result = jax.random.normal(stream_key, dims, jnp.float32) * deviation
    if len(cuts) > 0:
        result = levels(stream_key, dims, cuts, -0.22, 0.18) * result
    return jnp.clip(result, min=-reach, max=reach).astype(kind)


def setup_inputs(seed: int = 0, part: int = 0) -> dict:
    keys = jax.random.split(jax.random.key(seed), 11)
    part_splits = jax.random.split(jax.random.fold_in(keys[10], part), 11)
    return {
        "features": normal_values(part_splits[0], (POINTS, D), 1.0, 6.0, ((0, 128),)),
        "hilbert_rank": draw_hilbert_rank(jax.random.fold_in(jax.random.fold_in(keys[10], part), 71), part),
        "point_mask": set_ends((jax.random.randint(part_splits[2], (POINTS,), 0, 16) < 15).astype(jnp.int32), jax.random.fold_in(part_splits[2], 1), 0, 1),
        "norm_gains": jnp.clip(1.0 + 0.1 * jax.random.normal(keys[3], (5, D), jnp.float32), 0.5, 1.5).astype(jnp.bfloat16),
        "w_qkv": draw_w_qkv(jax.random.fold_in(keys[10], 71), part),
        "w_out": normal_values(keys[5], (2, D, D), D ** -0.5, 0.375),
        "w_up": normal_values(keys[6], (2, D, FF), D ** -0.5, 0.375),
        "w_down": normal_values(keys[7], (2, FF, D), FF ** -0.5, 0.1875),
        "head_hidden": normal_values(keys[8], (D, D), D ** -0.5, 0.375),
        "head_out": normal_values(keys[9], (D, OUTS), D ** -0.5, 0.375),
    }


EPS = 1e-05

def norm_rows(values, gain):
    center = values - lax.optimization_barrier(jnp.mean(values, axis=-1, keepdims=True))
    spread = lax.optimization_barrier(jnp.mean(center * center, axis=-1, keepdims=True))
    return center * lax.rsqrt(spread + EPS) * gain.astype(jnp.float32)

def attend_patch(patch, valid, gain, w_qkv, w_out):
    width = patch.shape[1]
    head_dim = width // HEADS
    normed = norm_rows(patch.astype(jnp.float32), gain).astype(jnp.bfloat16)
    qkv = jnp.dot(normed, w_qkv, preferred_element_type=jnp.float32).astype(jnp.bfloat16)
    keep = valid > 0

    def one_head(index):
        query = lax.dynamic_slice_in_dim(qkv, index * head_dim, head_dim, 1)
        random_keys = lax.dynamic_slice_in_dim(qkv, width + index * head_dim, head_dim, 1)
        vals = lax.dynamic_slice_in_dim(qkv, 2 * width + index * head_dim, head_dim, 1)
        scores = jnp.dot(query, random_keys.T, preferred_element_type=jnp.float32) * head_dim ** (-0.5)
        scores = jnp.where(keep[None, :], scores, -1e+30)
        top = lax.optimization_barrier(jnp.max(scores, axis=-1, keepdims=True))
        expo = jnp.exp(scores - top)
        weights = (expo / lax.optimization_barrier(jnp.sum(expo, axis=-1, keepdims=True))).astype(jnp.bfloat16)
        return jnp.dot(weights, vals, preferred_element_type=jnp.float32).astype(jnp.bfloat16)
    per_head = lax.map(one_head, jnp.arange(HEADS, dtype=jnp.int32))
    mixed = jnp.transpose(per_head, (1, 0, 2)).reshape(patch.shape)
    return patch.astype(jnp.float32) + jnp.dot(mixed, w_out, preferred_element_type=jnp.float32)

def run_block(rows, valid, gains, w_qkv, w_out, w_up, w_down):

    def one_patch(pair):
        patch, keep = pair
        middle = attend_patch(patch, keep, gains[0], w_qkv, w_out)
        normed = norm_rows(middle, gains[1]).astype(jnp.bfloat16)
        hidden = jax.nn.gelu(jnp.dot(normed, w_up, preferred_element_type=jnp.float32), approximate=False).astype(jnp.bfloat16)
        return (middle + jnp.dot(hidden, w_down, preferred_element_type=jnp.float32)).astype(jnp.bfloat16)
    patches = rows.reshape(-1, PATCH, rows.shape[1])
    masks = valid.reshape(-1, PATCH)
    return lax.map(one_patch, (patches, masks)).reshape(rows.shape)

def offset_head(rows, gain, head_hidden, head_out):
    normed = norm_rows(rows.astype(jnp.float32), gain).astype(jnp.bfloat16)
    inner = jax.nn.gelu(jnp.dot(normed, head_hidden, preferred_element_type=jnp.float32), approximate=False).astype(jnp.bfloat16)
    return jnp.dot(inner, head_out, preferred_element_type=jnp.float32)

def reference(features, hilbert_rank, point_mask, norm_gains, w_qkv, w_out, w_up, w_down, head_hidden, head_out):
    first = run_block(features, point_mask, norm_gains[0:2], w_qkv[0], w_out[0], w_up[0], w_down[0])
    ordered = jnp.zeros_like(first).at[hilbert_rank].set(first)
    ordered_mask = jnp.zeros_like(point_mask).at[hilbert_rank].set(point_mask)
    second = run_block(ordered, ordered_mask, norm_gains[2:4], w_qkv[1], w_out[1], w_up[1], w_down[1])
    home = second[hilbert_rank]
    return offset_head(home, norm_gains[4], head_hidden, head_out)
```

```python
import functools
import math

import jax
import jax.numpy as jnp
from jax import lax
from jax.experimental import pallas as pl
from jax.experimental.pallas import tpu as pltpu
from jax.sharding import PartitionSpec as P

HEADS = 16
WIDTH = 256
ROWS = 1024
HALF = 128
GROUP = 8
TILE = 256
QTILE = 512
EPS = 1e-05
LOG2E = math.log2(math.e)
SAFE = 64.0
LARGE = 1e30
F32 = jnp.float32
BF16 = jnp.bfloat16


def dot_nn(a, b):
    return lax.dot_general(a, b, (((1,), (0,)), ((), ())), preferred_element_type=F32)


def dot_nt(a, b):
    return lax.dot_general(a, b, (((1,), (1,)), ((), ())), preferred_element_type=F32)


def norm_rows(values, gain):
    center = values - jnp.mean(values, axis=-1, keepdims=True)
    spread = jnp.mean(center * center, axis=-1, keepdims=True)
    return center * lax.rsqrt(spread + EPS) * gain


def gelu(x):
    size = jnp.abs(x)
    t = 1.0 / (1.0 + (0.3275911 / math.sqrt(2.0)) * size)
    poly = t * (
        0.5 * 0.254829592
        + t
        * (
            -0.5 * 0.284496736
            + t * (0.5 * 1.421413741 + t * (-0.5 * 1.453152027 + t * (0.5 * 1.061405429)))
        )
    )
    tail = poly * jnp.exp2(x * x * (-0.5 * LOG2E))
    return jnp.maximum(x, 0.0) - size * tail


def tile_rows(i, size=TILE):
    return pl.ds(pl.multiple_of(i * size, size), size)


def run_block(x_ref, keep_ref, gains, wqkv_ref, wo_ref, wu_ref, wd_ref, out_ref, scratch):
    q_ref, k_ref, v_ref, m_ref = scratch
    any_valid = jnp.max(keep_ref[...], axis=(0, 1), keepdims=True)
    lane = lax.broadcasted_iota(jnp.int32, (1, 2 * HALF), 1)
    lane_head = (lane % HALF) // (WIDTH // HEADS)
    row_i = lax.broadcasted_iota(jnp.int32, (HALF, HALF), 0) // (WIDTH // HEADS)
    col_i = lax.broadcasted_iota(jnp.int32, (HALF, HALF), 1) // (WIDTH // HEADS)
    same = (row_i == col_i).astype(BF16)

    def project(i, carry):
        rows = tile_rows(i)
        normed = norm_rows(x_ref[rows, :].astype(F32), gains[0]).astype(BF16)
        qkv = dot_nn(normed, wqkv_ref[...]).astype(BF16)
        keep = jnp.where(any_valid > 0.0, keep_ref[rows, :], 1.0)
        scale = jnp.where(any_valid > 0.0, 0.25 * LOG2E, 0.0)
        out = []
        for g in range(2):
            lo_cols, hi_cols = slice(0, HALF), slice(HALF, 2 * HALF)
            q = qkv[:, HALF * g : HALF * (g + 1)].astype(F32) * scale
            high = q.astype(BF16)
            q_ref[g, rows, lo_cols] = high
            q_ref[g, rows, hi_cols] = (q - high.astype(F32)).astype(BF16)
            k = qkv[:, WIDTH + HALF * g : WIDTH + HALF * (g + 1)]
            k_ref[g, rows, lo_cols] = k
            k_ref[g, rows, hi_cols] = k
            v = qkv[:, 2 * WIDTH + HALF * g : 2 * WIDTH + HALF * (g + 1)].astype(F32)
            v_ref[g, rows, lo_cols] = (v * keep).astype(BF16)
            v_ref[g, rows, hi_cols] = jnp.broadcast_to(keep, (TILE, HALF)).astype(BF16)
            kf = k.astype(F32)
            for j, sq in ((0, q * q), (1, kf * kf)):
                top = jnp.max(dot_nn(jnp.minimum(sq, 10.0 * LARGE).astype(BF16), same), axis=0, keepdims=True)
                out.append(jnp.maximum(carry[2 * g + j], top))
        return tuple(out)

    tops = lax.fori_loop(0, ROWS // TILE, project, tuple(jnp.zeros((1, HALF), F32) for _ in range(4)))
    reach = jnp.max(jnp.maximum(tops[0] * tops[1], tops[2] * tops[3]))
    largest = jnp.max(jnp.maximum(jnp.maximum(tops[0], tops[1]), jnp.maximum(tops[2], tops[3])))
    safe = jnp.logical_and(reach < SAFE * SAFE, largest < LARGE)

    @pl.when(safe)
    def _():
        for g in range(2):

            def tile(i, carry):
                rows = tile_rows(i, QTILE)
                q = q_ref[g, rows, :]
                total = None
                for h in range(GROUP):
                    lanes = (lane_head == h).astype(BF16)
                    scores = dot_nt(q * lanes, k_ref[g])
                    part = dot_nn(jnp.exp2(scores).astype(BF16), v_ref[g] * lanes)
                    total = part if total is None else total + part
                m_ref[rows, HALF * g : HALF * (g + 1)] = (
                    total[:, 0:HALF] / total[:, HALF : 2 * HALF]
                ).astype(BF16)
                return carry

            lax.fori_loop(0, ROWS // QTILE, tile, 0)

    @pl.when(jnp.logical_not(safe))
    def _():
        pick = (lax.broadcasted_iota(jnp.int32, (8, 2 * HALF), 1) == HALF).astype(BF16)
        for g in range(2):

            def tile(i, carry):
                rows = tile_rows(i)

                def head(h, total):
                    lanes = (lane_head == h).astype(BF16)
                    keep_row = dot_nt(pick, v_ref[g])[0:1, :]
                    scores = dot_nt(q_ref[g, rows, :] * lanes, k_ref[g])
                    scores = jnp.where(keep_row > 0.0, scores, -1e30)
                    top = jnp.max(scores, axis=-1, keepdims=True)
                    expo = jnp.exp2(scores - top).astype(BF16)
                    return total + dot_nn(expo, v_ref[g] * lanes)

                total = lax.fori_loop(0, GROUP, head, jnp.zeros((TILE, 2 * HALF), F32))
                m_ref[rows, HALF * g : HALF * (g + 1)] = (
                    total[:, 0:HALF] / total[:, HALF : 2 * HALF]
                ).astype(BF16)
                return carry

            lax.fori_loop(0, ROWS // TILE, tile, 0)

    def mlp(i, carry):
        rows = tile_rows(i)
        middle = x_ref[rows, :].astype(F32) + dot_nn(m_ref[rows, :], wo_ref[...])
        normed = norm_rows(middle, gains[1]).astype(BF16)
        hidden = gelu(dot_nn(normed, wu_ref[...])).astype(BF16)
        out_ref[rows, :] = (middle + dot_nn(hidden, wd_ref[...])).astype(BF16)
        return carry

    lax.fori_loop(0, ROWS // TILE, mlp, 0)


def gains_of(gains_ref, *which):
    return [gains_ref[w : w + 1, :].astype(F32) for w in which]


def first_kernel(
    x_ref, keep_ref, pos_ref, gains_ref, wqkv_ref, wo_ref, wu_ref, wd_ref, send_ref, y_ref, *scratch
):
    gains = gains_of(gains_ref, 0, 1)
    weights = (wqkv_ref, wo_ref, wu_ref, wd_ref)
    run_block(x_ref, keep_ref, gains, *weights, y_ref, scratch)

    def pack(i, carry):
        slots = lax.broadcasted_iota(jnp.int32, (TILE, 1), 0) + i * TILE
        pick = (pos_ref[...] == slots).astype(F32).astype(BF16)
        send_ref[tile_rows(i), :] = dot_nn(pick, y_ref[...]).astype(BF16)
        return carry

    lax.fori_loop(0, send_ref.shape[0] // TILE, pack, 0)


def second_kernel(
    recv_ref, row_ref, col_ref, gains_ref, wqkv_ref, wo_ref, wu_ref, wd_ref, send_ref,
    x_ref, keep_ref, y_ref, *scratch
):
    def unpack(i, carry):
        slots = lax.broadcasted_iota(jnp.int32, (TILE, 1), 0) + i * TILE
        code = row_ref[...]
        valid = (code == 2 * slots + 1).astype(F32)
        pick = valid + (code == 2 * slots).astype(F32)
        x_ref[tile_rows(i), :] = dot_nn(pick.astype(BF16), recv_ref[...]).astype(BF16)
        keep_ref[tile_rows(i), :] = jnp.sum(valid, axis=1, keepdims=True)
        return carry

    lax.fori_loop(0, ROWS // TILE, unpack, 0)
    gains = gains_of(gains_ref, 2, 3)
    weights = (wqkv_ref, wo_ref, wu_ref, wd_ref)
    run_block(x_ref, keep_ref, gains, *weights, y_ref, scratch)

    def pack(i, carry):
        slots = 2 * lax.broadcasted_iota(jnp.int32, (1, ROWS), 1)
        code = col_ref[tile_rows(i), :]
        pick = ((code == slots) | (code == slots + 1)).astype(F32).astype(BF16)
        send_ref[tile_rows(i), :] = dot_nn(pick, y_ref[...]).astype(BF16)
        return carry

    lax.fori_loop(0, send_ref.shape[0] // TILE, pack, 0)


def head_kernel(recv_ref, pos_ref, gains_ref, hidden_ref, out_w_ref, out_ref):
    gain = gains_of(gains_ref, 4)[0]

    def tile(i, carry):
        slots = lax.broadcasted_iota(jnp.int32, (1, recv_ref.shape[0]), 1)
        pick = (pos_ref[tile_rows(i), :] == slots).astype(F32).astype(BF16)
        home = dot_nn(pick, recv_ref[...])
        normed = norm_rows(home, gain).astype(BF16)
        inner = gelu(dot_nn(normed, hidden_ref[...])).astype(BF16)
        out_ref[tile_rows(i), :] = dot_nn(inner, out_w_ref[...])
        return carry

    lax.fori_loop(0, ROWS // TILE, tile, 0)


VMEM = pl.BlockSpec(memory_space=pltpu.VMEM)
BLOCK_SCRATCH = [pltpu.VMEM((2, ROWS, WIDTH), BF16)] * 3 + [pltpu.VMEM((ROWS, WIDTH), BF16)]
PARAMS = pltpu.CompilerParams(vmem_limit_bytes=48 * 2**20)


def call(kernel, shape, dtype, scratch, *args):
    return pl.pallas_call(
        kernel,
        out_shape=jax.ShapeDtypeStruct(shape, dtype),
        in_specs=[VMEM] * len(args),
        out_specs=VMEM,
        scratch_shapes=scratch,
        compiler_params=PARAMS,
    )(*args)


def body(
    features, hilbert_rank, point_mask, norm_gains, w_qkv, w_out, w_up, w_down, head_hidden, head_out
):
    count = features.shape[0]
    peers = lax.axis_size("pts")
    room = 2 * count // peers
    slots = peers * room
    target = hilbert_rank // count
    slot = hilbert_rank % count
    onehot = (target[:, None] == jnp.arange(peers, dtype=jnp.int32)[None, :]).astype(jnp.int32)
    within = jnp.sum(jnp.cumsum(onehot, axis=0) * onehot, axis=1) - 1
    position = target * room + within
    send_code = jnp.full((slots,), -1, jnp.int32).at[position].set(slot * 2 + point_mask)
    recv_code = lax.all_to_all(send_code, "pts", split_axis=0, concat_axis=0, tiled=True)
    keep = (point_mask > 0).astype(F32)[:, None]
    row = pltpu.VMEM((count, WIDTH), BF16)
    send = call(
        first_kernel, (slots, WIDTH), BF16, [row] + BLOCK_SCRATCH,
        features, keep, position[None, :], norm_gains, w_qkv[0], w_out[0], w_up[0], w_down[0],
    )
    recv = lax.all_to_all(send, "pts", split_axis=0, concat_axis=0, tiled=True)
    send = call(
        second_kernel, (slots, WIDTH), BF16, [row, pltpu.VMEM((count, 1), F32), row] + BLOCK_SCRATCH,
        recv, recv_code[None, :], recv_code[:, None], norm_gains, w_qkv[1], w_out[1], w_up[1], w_down[1],
    )
    recv = lax.all_to_all(send, "pts", split_axis=0, concat_axis=0, tiled=True)
    return call(
        head_kernel, (count, head_out.shape[1]), F32, [],
        recv, position[:, None], norm_gains, head_hidden, head_out,
    )


def solution(mesh):
    spread = P(("rep", "pts"))
    in_specs = (P(("rep", "pts"), None), spread, spread) + (P(),) * 7
    return jax.shard_map(
        body, mesh=mesh, in_specs=in_specs, out_specs=P(("rep", "pts"), None), check_vma=False
    )
```

```python
import math

import jax
import jax.numpy as jnp
from jax import lax
from jax.experimental import pallas as pl
from jax.experimental.pallas import tpu as pltpu
from jax.sharding import PartitionSpec as P

PEERS = 128
ROOM = 16
ROWS = 1024
SLOTS = PEERS * ROOM
WIDTH = 256
HALF = 128
QUART = 64
DEPTH = 16
FF = 1024
OUTS = 4
TILE = 256
STEP = TILE // ROOM
TILES = ROWS // TILE
EPS = 1e-05
LOG2E = math.log2(math.e)
F32 = jnp.float32
BF16 = jnp.bfloat16
MESH = pl.DeviceIdType.MESH


def dot_nn(a, b):
    return lax.dot_general(a, b, (((1,), (0,)), ((), ())), preferred_element_type=F32)


def dot_nt(a, b):
    return lax.dot_general(a, b, (((1,), (1,)), ((), ())), preferred_element_type=F32)


def dot_tn(a, b):
    return lax.dot_general(a, b, (((0,), (0,)), ((), ())), preferred_element_type=F32)


def iota(shape, dim):
    return lax.broadcasted_iota(jnp.int32, shape, dim)


def ones_where(test):
    return jnp.where(test, 1.0, 0.0)


def norm_rows(values, gain):
    center = values - jnp.mean(values, axis=-1, keepdims=True)
    spread = jnp.mean(center * center, axis=-1, keepdims=True)
    return center * lax.rsqrt(spread + EPS) * gain


def gelu(x):
    size = jnp.abs(x)
    t = 1.0 / (1.0 + (0.3275911 / math.sqrt(2.0)) * size)
    poly = t * (
        0.5 * 0.254829592
        + t
        * (
            -0.5 * 0.284496736
            + t * (0.5 * 1.421413741 + t * (-0.5 * 1.453152027 + t * (0.5 * 1.061405429)))
        )
    )
    tail = poly * jnp.exp2(x * x * (-0.5 * LOG2E))
    return jnp.maximum(x, 0.0) - size * tail


def tile_rows(i, size=TILE):
    return pl.ds(pl.multiple_of(i * size, size), size)


def to_column(row):
    return jnp.transpose(jnp.broadcast_to(row, (HALF, row.shape[1])))[:, 0:1]


def starts_of(counts):
    below = ones_where(iota((PEERS, PEERS), 1) < iota((PEERS, PEERS), 0)).astype(BF16)
    wide = jnp.broadcast_to(counts, (PEERS, HALF)).astype(BF16)
    return dot_nn(below, wide)[:, 0:1]


def slots_of(counts, starts):
    place = iota((1, ROWS), 1).astype(F32)
    block = jnp.sum(ones_where(starts + counts <= place), axis=0, keepdims=True)
    begin = jnp.max(jnp.where(starts <= place, starts, 0.0), axis=0, keepdims=True)
    return block, place - begin


def project(x_ref, keep_ref, any_valid, gain, wqkv, q_ref, k_ref, v_ref):
    scale = jnp.where(any_valid > 0.0, 0.25 * LOG2E, 0.0)
    first_lane = iota((1, HALF), 1) == 0
    flag = jnp.broadcast_to(ones_where(first_lane), (TILE, HALF)).astype(BF16)

    def chunk(i, carry):
        rows = tile_rows(i)
        normed = norm_rows(x_ref[rows, :].astype(F32), gain).astype(BF16)
        qkv = dot_nn(normed, wqkv[...]).astype(BF16)
        drop = jnp.where(jnp.logical_and(any_valid > 0.0, keep_ref[rows, :] < 0.5), -1e30, 0.0)
        bias = jnp.where(first_lane, drop, 0.0).astype(BF16)
        for g in range(4):
            q = qkv[:, QUART * g : QUART * (g + 1)].astype(F32) * scale
            high = q.astype(BF16)
            low = (q - high.astype(F32)).astype(BF16)
            k = qkv[:, WIDTH + QUART * g : WIDTH + QUART * (g + 1)]
            q_ref[g, rows, 0:HALF] = jnp.concatenate([high, low], axis=1)
            q_ref[g, rows, HALF:WIDTH] = flag
            k_ref[g, rows, 0:HALF] = jnp.concatenate([k, k], axis=1)
            k_ref[g, rows, HALF:WIDTH] = bias
        for g in range(2):
            v_ref[g, rows, 0:HALF] = qkv[:, 2 * WIDTH + HALF * g : 2 * WIDTH + HALF * (g + 1)]
            v_ref[g, rows, HALF:WIDTH] = jnp.ones((TILE, HALF), BF16)
        return carry

    lax.fori_loop(0, TILES, chunk, 0)


def attend(rows, q_ref, k_ref, v_ref):
    lane = iota((1, WIDTH), 1)
    both = []
    for g in range(2):
        total = None
        for h in range(8):
            quad, inner = 2 * g + h // 4, h % 4
            mine = jnp.logical_or(
                jnp.logical_and(lane < HALF, (lane % QUART) // DEPTH == inner), lane == HALF
            )
            query = q_ref[quad, rows, :] * ones_where(mine).astype(BF16)
            scores = dot_nt(query, k_ref[quad])
            top = jnp.max(scores, axis=-1, keepdims=True)
            expo = jnp.exp2(scores - top).astype(BF16)
            picked = ones_where((lane % HALF) // DEPTH == h).astype(BF16)
            part = dot_nn(expo, v_ref[g] * picked)
            total = part if total is None else total + part
        both.append((total[:, 0:HALF] / total[:, HALF:WIDTH]).astype(BF16))
    return jnp.concatenate(both, axis=1)


def finish(x, mixed, gain, wo, wu, wd):
    middle = x.astype(F32) + dot_nn(mixed, wo[...])
    normed = norm_rows(middle, gain).astype(BF16)
    hidden = gelu(dot_nn(normed, wu[...])).astype(BF16)
    return (middle + dot_nn(hidden, wd[...])).astype(BF16)


def kernel(
    rank_ref, mask_ref, gains_ref, x_hbm, wqkv_hbm, wo_hbm, wu_hbm, wd_hbm, hh_hbm, ho_hbm, out_ref,
    x_ref, wqkv, wo, wu, wd, hh, ho, xs_ref, keep_ref, q_ref, k_ref, v_ref, y_ref,
    slot_ref, codes, got_codes, pick_ref, send1, recv1, send2, recv2, load_sem, send_sem, recv_sem,
):
    me = lax.axis_index("pts")
    barrier = pltpu.get_barrier_semaphore()

    def greet(k, carry):
        peer = lax.rem(me + k, PEERS)
        pl.semaphore_signal(barrier, inc=1, device_id={"pts": peer}, device_id_type=MESH)
        return carry

    lax.fori_loop(1, PEERS, greet, 0)
    loads = [
        pltpu.make_async_copy(source, target, load_sem.at[n])
        for n, (source, target) in enumerate(
            (
                (x_hbm, x_ref), (wqkv_hbm, wqkv), (wo_hbm, wo), (wu_hbm, wu), (wd_hbm, wd),
                (hh_hbm, hh), (ho_hbm, ho),
            )
        )
    ]
    for load in loads:
        load.start()

    def gain(n):
        return gains_ref[n : n + 1, :].astype(F32)

    def send_blocks(which, source, target, low, high, sign):
        def one(k, carry):
            rows = pl.ds(pl.multiple_of(k * ROOM, ROOM), ROOM)
            pltpu.make_async_remote_copy(
                src_ref=source.at[rows], dst_ref=target.at[rows],
                send_sem=send_sem.at[which], recv_sem=recv_sem.at[which],
                device_id={"pts": lax.rem(me + PEERS + sign * k, PEERS)}, device_id_type=MESH,
            ).start()
            return carry

        lax.fori_loop(low, high, one, 0)

    def keep_own(which, source, target):
        rows = pl.ds(0, ROOM)
        pltpu.make_async_copy(source.at[rows], target.at[rows], recv_sem.at[which]).start()

    def wait_sent(which, source, target):
        rows = pl.ds(0, SLOTS - ROOM)
        pltpu.make_async_copy(source.at[rows], target.at[rows], send_sem.at[which]).wait()

    def wait_received(which, source, target):
        pltpu.make_async_copy(source, target, recv_sem.at[which]).wait()

    block = ((rank_ref[...] // ROWS - me + PEERS) % PEERS).astype(F32)
    valid = ones_where(mask_ref[...] > 0)
    hot = ones_where(iota((PEERS, 1), 0).astype(F32) == block)
    counts = jnp.sum(hot, axis=1, keepdims=True)
    starts = starts_of(counts)
    earlier = ones_where(iota((ROWS, ROWS), 0) < iota((ROWS, ROWS), 1)).astype(BF16)
    before = dot_nn(hot.astype(BF16), earlier)
    within = jnp.sum(hot * before, axis=0, keepdims=True)
    place = within + jnp.sum(hot * starts, axis=0, keepdims=True)
    home_slot = to_column(block * ROOM + within)
    marks = jnp.where(iota((HALF, 1), 0).astype(F32) == within, 1.0 + valid, 0.0)
    codes[...] = dot_nt(hot.astype(BF16), marks.astype(BF16))
    sorted_block, sorted_within = slots_of(counts, starts)
    slot_ref[...] = sorted_block * ROOM + sorted_within
    y_ref[...] = jnp.zeros((ROWS, WIDTH), BF16)
    loads[0].wait()

    def sort(i, carry):
        want = (iota((TILE, 1), 0) + i * TILE).astype(F32)
        pick = ones_where(want == place)
        xs_ref[tile_rows(i), :] = dot_nn(pick.astype(BF16), x_ref[...]).astype(BF16)
        keep_ref[tile_rows(i), :] = jnp.sum(pick * valid, axis=1, keepdims=True)
        return carry

    lax.fori_loop(0, TILES, sort, 0)
    for load in loads[1:]:
        load.wait()

    def pack(i, send_ref):
        slot = (iota((TILE, 1), 0) + i * TILE).astype(F32)
        pick = ones_where(slot == slot_ref[...]).astype(BF16)
        send_ref[tile_rows(i), :] = dot_nn(pick, y_ref[...]).astype(BF16)

    def run_block(index, any_valid, send_ref, recv_ref, which, sign):
        weights = (wo.at[index], wu.at[index], wd.at[index])
        project(
            xs_ref, keep_ref, any_valid, gain(2 * index), wqkv.at[index], q_ref, k_ref, v_ref
        )

        def work(i):
            rows = tile_rows(i)
            mixed = attend(rows, q_ref, k_ref, v_ref)
            y_ref[rows, :] = finish(xs_ref[rows, :], mixed, gain(2 * index + 1), *weights)
            pack(i, send_ref)

        work(0)
        if index == 0:
            pl.semaphore_wait(barrier, PEERS - 1)

            def one(k, carry):
                row = pl.ds(k, 1)
                pltpu.make_async_remote_copy(
                    src_ref=codes.at[row], dst_ref=got_codes.at[row],
                    send_sem=send_sem.at[2], recv_sem=recv_sem.at[2],
                    device_id={"pts": lax.rem(me + k, PEERS)}, device_id_type=MESH,
                ).start()
                return carry

            lax.fori_loop(1, PEERS, one, 0)
            row = pl.ds(0, 1)
            pltpu.make_async_copy(codes.at[row], got_codes.at[row], recv_sem.at[2]).start()
        keep_own(which, send_ref, recv_ref)
        send_blocks(which, send_ref, recv_ref, 1, STEP, sign)

        def later(i, carry):
            work(i)
            send_blocks(which, send_ref, recv_ref, STEP * i, STEP * i + STEP, sign)
            return carry

        lax.fori_loop(1, TILES, later, 0)

        def rest(i, carry):
            pack(i, send_ref)
            send_blocks(which, send_ref, recv_ref, STEP * i, STEP * i + STEP, sign)
            return carry

        lax.fori_loop(TILES, SLOTS // TILE, rest, 0)

    run_block(0, jnp.max(valid, axis=(0, 1), keepdims=True), send1, recv1, 0, 1)

    pltpu.make_async_copy(codes, got_codes, recv_sem.at[2]).wait()
    wait_codes = pl.ds(0, PEERS - 1)
    pltpu.make_async_copy(codes.at[wait_codes], got_codes.at[wait_codes], send_sem.at[2]).wait()
    code = got_codes[...]
    counts2 = jnp.sum(ones_where(code > 0.5), axis=1, keepdims=True)
    starts2 = starts_of(counts2)
    block2, within2 = slots_of(counts2, starts2)
    slot2 = block2 * ROOM + within2
    slot_ref[...] = slot2
    hot2 = ones_where(iota((PEERS, 1), 0).astype(F32) == block2).astype(BF16)
    marks2 = dot_tn(code.astype(BF16), hot2)
    mark = jnp.where(iota((HALF, 1), 0).astype(F32) == within2, marks2, 0.0)
    valid2 = ones_where(jnp.sum(mark, axis=0, keepdims=True) > 1.5)
    keep_ref[...] = to_column(valid2)
    slot_column = to_column(slot2)
    lanes = iota((1, SLOTS), 1).astype(F32)
    pick_ref[...] = ones_where(slot_column == lanes).astype(BF16)
    wait_received(0, send1, recv1)

    def unpack(i, carry):
        xs_ref[tile_rows(i), :] = dot_nn(pick_ref[tile_rows(i), :], recv1[...]).astype(BF16)
        return carry

    lax.fori_loop(0, TILES, unpack, 0)
    run_block(1, jnp.max(valid2, axis=(0, 1), keepdims=True), send2, recv2, 1, -1)

    pick_ref[...] = ones_where(home_slot == lanes).astype(BF16)
    wait_sent(0, send1, recv1)
    wait_received(1, send2, recv2)

    def head(i, carry):
        home = dot_nn(pick_ref[tile_rows(i), :], recv2[...])
        normed = norm_rows(home, gain(4)).astype(BF16)
        inner = gelu(dot_nn(normed, hh[...])).astype(BF16)
        out_ref[tile_rows(i), :] = dot_nn(inner, ho[...])
        return carry

    lax.fori_loop(0, TILES, head, 0)
    wait_sent(1, send2, recv2)


def body(
    features, hilbert_rank, point_mask, norm_gains, w_qkv, w_out, w_up, w_down, head_hidden, head_out
):
    vmem = pl.BlockSpec(memory_space=pltpu.VMEM)
    away = pl.BlockSpec(memory_space=pl.ANY)
    rows = pltpu.VMEM((ROWS, WIDTH), BF16)
    slots = pltpu.VMEM((SLOTS, WIDTH), BF16)
    return pl.pallas_call(
        kernel,
        out_shape=jax.ShapeDtypeStruct((ROWS, OUTS), F32),
        in_specs=[vmem] * 3 + [away] * 7,
        out_specs=vmem,
        scratch_shapes=[
            rows,
            pltpu.VMEM((2, WIDTH, 3 * WIDTH), BF16),
            pltpu.VMEM((2, WIDTH, WIDTH), BF16),
            pltpu.VMEM((2, WIDTH, FF), BF16),
            pltpu.VMEM((2, FF, WIDTH), BF16),
            pltpu.VMEM((WIDTH, WIDTH), BF16),
            pltpu.VMEM((WIDTH, OUTS), BF16),
            rows,
            pltpu.VMEM((ROWS, 1), F32),
            pltpu.VMEM((4, ROWS, WIDTH), BF16),
            pltpu.VMEM((4, ROWS, WIDTH), BF16),
            pltpu.VMEM((2, ROWS, WIDTH), BF16),
            rows,
            pltpu.VMEM((1, ROWS), F32),
            pltpu.VMEM((PEERS, HALF), F32),
            pltpu.VMEM((PEERS, HALF), F32),
            pltpu.VMEM((ROWS, SLOTS), BF16),
            slots,
            slots,
            slots,
            slots,
            pltpu.SemaphoreType.DMA((7,)),
            pltpu.SemaphoreType.DMA((3,)),
            pltpu.SemaphoreType.DMA((3,)),
        ],
        compiler_params=pltpu.CompilerParams(
            collective_id=0, has_side_effects=True, vmem_limit_bytes=56 * 2**20
        ),
    )(
        hilbert_rank[None, :], point_mask[None, :], norm_gains, features, w_qkv, w_out, w_up, w_down,
        head_hidden, head_out,
    )


def solution(mesh):
    spread = P(("rep", "pts"))
    in_specs = (P(("rep", "pts"), None), spread, spread) + (P(),) * 7
    return jax.shard_map(
        body, mesh=mesh, in_specs=in_specs, out_specs=P(("rep", "pts"), None), check_vma=False
    )
```

```python
import math

import jax
import jax.numpy as jnp
from jax import lax
from jax.experimental import pallas as pl
from jax.experimental.pallas import tpu as pltpu
from jax.sharding import PartitionSpec as P

PEERS = 128
ROOM = 16
ROWS = 1024
SLOTS = PEERS * ROOM
WIDTH = 256
HALF = 128
QUART = 64
DEPTH = 16
FF = 1024
OUTS = 4
TILE = 256
STEP = TILE // ROOM
TILES = ROWS // TILE
EPS = 1e-05
LOG2E = math.log2(math.e)
F32 = jnp.float32
BF16 = jnp.bfloat16
MESH = pl.DeviceIdType.MESH


def dot_nn(a, b):
    return lax.dot_general(a, b, (((1,), (0,)), ((), ())), preferred_element_type=F32)


def dot_nt(a, b):
    return lax.dot_general(a, b, (((1,), (1,)), ((), ())), preferred_element_type=F32)


def dot_tn(a, b):
    return lax.dot_general(a, b, (((0,), (0,)), ((), ())), preferred_element_type=F32)


def iota(shape, dim):
    return lax.broadcasted_iota(jnp.int32, shape, dim)


def ones_where(test):
    return jnp.where(test, 1.0, 0.0)


def norm_rows(values, gain):
    center = values - jnp.mean(values, axis=-1, keepdims=True)
    spread = jnp.mean(center * center, axis=-1, keepdims=True)
    return center * lax.rsqrt(spread + EPS) * gain


def gelu(x):
    size = jnp.abs(x)
    t = 1.0 / (1.0 + (0.3275911 / math.sqrt(2.0)) * size)
    poly = t * (
        0.5 * 0.254829592
        + t
        * (
            -0.5 * 0.284496736
            + t * (0.5 * 1.421413741 + t * (-0.5 * 1.453152027 + t * (0.5 * 1.061405429)))
        )
    )
    tail = poly * jnp.exp2(x * x * (-0.5 * LOG2E))
    return jnp.maximum(x, 0.0) - size * tail


def tile_rows(i, size=TILE):
    return pl.ds(pl.multiple_of(i * size, size), size)


def to_column(row):
    return jnp.transpose(jnp.broadcast_to(row, (HALF, row.shape[1])))[:, 0:1]


def starts_of(counts):
    below = ones_where(iota((PEERS, PEERS), 1) < iota((PEERS, PEERS), 0)).astype(BF16)
    wide = jnp.broadcast_to(counts, (PEERS, HALF)).astype(BF16)
    return dot_nn(below, wide)[:, 0:1]


def slots_of(counts, starts):
    place = iota((1, ROWS), 1).astype(F32)
    block = jnp.sum(ones_where(starts + counts <= place), axis=0, keepdims=True)
    begin = jnp.max(jnp.where(starts <= place, starts, 0.0), axis=0, keepdims=True)
    return block, place - begin


def project(x_ref, keep_ref, any_valid, gain, wqkv, q_ref, k_ref, v_ref):
    scale = jnp.where(any_valid > 0.0, 0.25 * LOG2E, 0.0)
    first_lane = iota((1, HALF), 1) == 0
    flag = jnp.broadcast_to(ones_where(first_lane), (TILE, HALF)).astype(BF16)

    def chunk(i, carry):
        rows = tile_rows(i)
        normed = norm_rows(x_ref[rows, :].astype(F32), gain).astype(BF16)
        qkv = dot_nn(normed, wqkv[...]).astype(BF16)
        drop = jnp.where(jnp.logical_and(any_valid > 0.0, keep_ref[rows, :] < 0.5), -1e30, 0.0)
        bias = jnp.where(first_lane, drop, 0.0).astype(BF16)
        for g in range(4):
            q = qkv[:, QUART * g : QUART * (g + 1)].astype(F32) * scale
            high = q.astype(BF16)
            low = (q - high.astype(F32)).astype(BF16)
            k = qkv[:, WIDTH + QUART * g : WIDTH + QUART * (g + 1)]
            q_ref[g, rows, 0:HALF] = jnp.concatenate([high, low], axis=1)
            q_ref[g, rows, HALF:WIDTH] = flag
            k_ref[g, rows, 0:HALF] = jnp.concatenate([k, k], axis=1)
            k_ref[g, rows, HALF:WIDTH] = bias
        for g in range(2):
            v_ref[g, rows, 0:HALF] = qkv[:, 2 * WIDTH + HALF * g : 2 * WIDTH + HALF * (g + 1)]
            v_ref[g, rows, HALF:WIDTH] = jnp.ones((TILE, HALF), BF16)
        return carry

    lax.fori_loop(0, TILES, chunk, 0)


def attend(rows, q_ref, k_ref, v_ref, between=()):
    lane = iota((1, WIDTH), 1)
    steps = list(between)

    def scores_of(n):
        quad, inner = n // 4, n % 4
        mine = jnp.logical_or(
            jnp.logical_and(lane < HALF, (lane % QUART) // DEPTH == inner), lane == HALF
        )
        query = q_ref[quad, rows, :] * ones_where(mine).astype(BF16)
        return dot_nt(query, k_ref[quad])

    both = []
    scores = scores_of(0)
    for g in range(2):
        total = None
        for h in range(8):
            n = 8 * g + h
            following = scores_of(n + 1) if n < 15 else None
            top = jnp.max(scores, axis=-1, keepdims=True)
            expo = jnp.exp2(scores - top).astype(BF16)
            picked = ones_where((lane % HALF) // DEPTH == h).astype(BF16)
            part = dot_nn(expo, v_ref[g] * picked)
            total = part if total is None else total + part
            scores = following
            if steps:
                steps.pop(0)()
        both.append((total[:, 0:HALF] / total[:, HALF:WIDTH]).astype(BF16))
    return jnp.concatenate(both, axis=1)


def finish_steps(x_ref, m_ref, y_ref, rows, gain, wo, wu, wd):
    held = {}

    def begin():
        held["sum"] = x_ref[rows, :].astype(F32) + dot_nn(m_ref[rows, :], wo[...])
        held["normed"] = norm_rows(held["sum"], gain).astype(BF16)

    def part(c):
        def step():
            hidden = gelu(dot_nn(held["normed"], wu[:, WIDTH * c : WIDTH * (c + 1)])).astype(BF16)
            held["sum"] = held["sum"] + dot_nn(hidden, wd[WIDTH * c : WIDTH * (c + 1), :])

        return step

    def end():
        y_ref[rows, :] = held["sum"].astype(BF16)

    return [begin] + [part(c) for c in range(FF // WIDTH)] + [end]


def kernel(
    rank_ref, mask_ref, gains_ref, ho, x_hbm, wqkv_hbm, wo_hbm, wu_hbm, wd_hbm, hh_hbm, out_ref,
    x_ref, wqkv, wo, wu, wd, hh, xs_ref, keep_ref, q_ref, k_ref, v_ref, m_ref, y_ref,
    slot_ref, codes, got_codes, pick_ref, send1, recv1, send2, recv2, load_sem, send_sem, recv_sem,
    go_sem,
):
    me = lax.axis_index("pts")
    rep = lax.axis_index("rep")
    loads = [
        pltpu.make_async_copy(source, target, load_sem.at[n])
        for n, (source, target) in enumerate(
            (
                (x_hbm, x_ref), (wqkv_hbm, wqkv), (wo_hbm, wo), (wu_hbm, wu), (wd_hbm, wd),
                (hh_hbm, hh),
            )
        )
    ]
    for load in loads:
        load.start()

    barrier = pltpu.get_barrier_semaphore()

    def greet(k, carry):
        peer = lax.rem(me + k, PEERS)
        pl.semaphore_signal(barrier, inc=1, device_id={"pts": peer}, device_id_type=MESH)
        return carry

    lax.fori_loop(1, PEERS, greet, 0)
    partner = {"rep": 1 - rep}
    pl.semaphore_signal(barrier, inc=1, device_id=partner, device_id_type=MESH)

    def gain(n):
        return gains_ref[n : n + 1, :].astype(F32)

    def send_blocks(which, source, target, low, high, sign):
        def one(k, carry):
            rows = pl.ds(pl.multiple_of(k * ROOM, ROOM), ROOM)
            pltpu.make_async_remote_copy(
                src_ref=source.at[rows], dst_ref=target.at[rows],
                send_sem=send_sem.at[which], recv_sem=recv_sem.at[which],
                device_id={"pts": lax.rem(me + PEERS + sign * k, PEERS)}, device_id_type=MESH,
            ).start()
            return carry

        lax.fori_loop(low, high, one, 0)

    def keep_own(which, source, target):
        rows = pl.ds(0, ROOM)
        pltpu.make_async_copy(source.at[rows], target.at[rows], recv_sem.at[which]).start()

    def wait_sent(which, source, target):
        rows = pl.ds(0, SLOTS - ROOM)
        pltpu.make_async_copy(source.at[rows], target.at[rows], send_sem.at[which]).wait()

    def wait_received(which, source, target):
        pltpu.make_async_copy(source, target, recv_sem.at[which]).wait()

    block = ((rank_ref[...] // ROWS - me + PEERS) % PEERS).astype(F32)
    valid = ones_where(mask_ref[...] > 0)
    hot = ones_where(iota((PEERS, 1), 0).astype(F32) == block)
    counts = jnp.sum(hot, axis=1, keepdims=True)
    starts = starts_of(counts)
    earlier = ones_where(iota((ROWS, ROWS), 0) < iota((ROWS, ROWS), 1)).astype(BF16)
    before = dot_nn(hot.astype(BF16), earlier)
    within = jnp.sum(hot * before, axis=0, keepdims=True)
    place = within + jnp.sum(hot * starts, axis=0, keepdims=True)
    home_slot = to_column(block * ROOM + within)
    marks = jnp.where(iota((HALF, 1), 0).astype(F32) == within, 1.0 + valid, 0.0)
    codes[...] = dot_nt(hot.astype(BF16), marks.astype(BF16))
    sorted_block, sorted_within = slots_of(counts, starts)
    slot_ref[...] = sorted_block * ROOM + sorted_within
    y_ref[...] = jnp.zeros((ROWS, WIDTH), BF16)
    loads[0].wait()

    def sort(i, carry):
        want = (iota((TILE, 1), 0) + i * TILE).astype(F32)
        pick = ones_where(want == place)
        xs_ref[tile_rows(i), :] = dot_nn(pick.astype(BF16), x_ref[...]).astype(BF16)
        keep_ref[tile_rows(i), :] = jnp.sum(pick * valid, axis=1, keepdims=True)
        return carry

    lax.fori_loop(0, TILES, sort, 0)
    for load in loads[1:]:
        load.wait()

    def pack(i, send_ref):
        slot = (iota((TILE, 1), 0) + i * TILE).astype(F32)
        pick = ones_where(slot == slot_ref[...]).astype(BF16)
        send_ref[tile_rows(i), :] = dot_nn(pick, y_ref[...]).astype(BF16)

    def send_step(i, send_ref, recv_ref, which, sign):
        low = STEP * i + (TILES - 2 - i) // (TILES - 2)
        send_blocks(which, send_ref, recv_ref, low, STEP * (i + 1), sign)

    def run_block(index, any_valid, send_ref, recv_ref, which, sign):
        weights = (wo.at[index], wu.at[index], wd.at[index])
        project(
            xs_ref, keep_ref, any_valid, gain(2 * index), wqkv.at[index], q_ref, k_ref, v_ref
        )

        def steps(i):
            rest = finish_steps(
                xs_ref, m_ref, y_ref, tile_rows(i), gain(2 * index + 1), *weights
            )
            return rest + [lambda: pack(i, send_ref)]

        m_ref[tile_rows(0), :] = attend(tile_rows(0), q_ref, k_ref, v_ref)
        if index == 0:
            pl.semaphore_wait(barrier, PEERS)

            def one(k, carry):
                row = pl.ds(k, 1)
                pltpu.make_async_remote_copy(
                    src_ref=codes.at[row], dst_ref=got_codes.at[row],
                    send_sem=send_sem.at[2], recv_sem=recv_sem.at[2],
                    device_id={"pts": lax.rem(me + k, PEERS)}, device_id_type=MESH,
                ).start()
                return carry

            lax.fori_loop(1, PEERS, one, 0)
            row = pl.ds(0, 1)
            pltpu.make_async_copy(codes.at[row], got_codes.at[row], recv_sem.at[2]).start()

        def later(i, carry):
            between = steps(i - 1) + [lambda: send_step(i - 1, send_ref, recv_ref, which, sign)]
            m_ref[tile_rows(i), :] = attend(tile_rows(i), q_ref, k_ref, v_ref, between)
            return carry

        lax.fori_loop(1, TILES, later, 0)
        keep_own(which, send_ref, recv_ref)
        for step in steps(TILES - 1):
            step()

    def send_rest(send_ref, recv_ref, which, sign):
        send_blocks(which, send_ref, recv_ref, STEP * (TILES - 1), STEP * TILES, sign)

        def rest(i, carry):
            pack(i, send_ref)
            send_blocks(which, send_ref, recv_ref, STEP * i, STEP * i + STEP, sign)
            return carry

        lax.fori_loop(TILES, SLOTS // TILE, rest, 0)

    run_block(0, jnp.max(valid, axis=(0, 1), keepdims=True), send1, recv1, 0, 1)

    @pl.when(rep == 0)
    def _():
        send_rest(send1, recv1, 0, 1)

    @pl.when(rep == 1)
    def _():
        def rest(i, carry):
            pack(i, send1)
            return carry

        lax.fori_loop(TILES, SLOTS // TILE, rest, 0)

    pltpu.make_async_copy(codes, got_codes, recv_sem.at[2]).wait()
    wait_codes = pl.ds(0, PEERS - 1)
    pltpu.make_async_copy(codes.at[wait_codes], got_codes.at[wait_codes], send_sem.at[2]).wait()
    code = got_codes[...]
    counts2 = jnp.sum(ones_where(code > 0.5), axis=1, keepdims=True)
    starts2 = starts_of(counts2)
    block2, within2 = slots_of(counts2, starts2)
    slot2 = block2 * ROOM + within2
    slot_ref[...] = slot2
    hot2 = ones_where(iota((PEERS, 1), 0).astype(F32) == block2).astype(BF16)
    marks2 = dot_tn(code.astype(BF16), hot2)
    mark = jnp.where(iota((HALF, 1), 0).astype(F32) == within2, marks2, 0.0)
    valid2 = ones_where(jnp.sum(mark, axis=0, keepdims=True) > 1.5)
    keep_ref[...] = to_column(valid2)
    slot_column = to_column(slot2)
    lanes = iota((1, SLOTS), 1).astype(F32)
    pick_ref[...] = ones_where(slot_column == lanes).astype(BF16)

    @pl.when(rep == 0)
    def _():
        wait_sent(0, send1, recv1)
        pl.semaphore_signal(go_sem, inc=1, device_id=partner, device_id_type=MESH)

    @pl.when(rep == 1)
    def _():
        pl.semaphore_wait(go_sem, 1)
        send_blocks(0, send1, recv1, STEP * (TILES - 1), PEERS, 1)

    wait_received(0, send1, recv1)

    def unpack(i, carry):
        xs_ref[tile_rows(i), :] = dot_nn(pick_ref[tile_rows(i), :], recv1[...]).astype(BF16)
        return carry

    lax.fori_loop(0, TILES, unpack, 0)
    run_block(1, jnp.max(valid2, axis=(0, 1), keepdims=True), send2, recv2, 1, -1)
    send_rest(send2, recv2, 1, -1)

    pick_ref[...] = ones_where(home_slot == lanes).astype(BF16)

    @pl.when(rep == 1)
    def _():
        wait_sent(0, send1, recv1)

    wait_received(1, send2, recv2)

    def head(i, carry):
        home = dot_nn(pick_ref[tile_rows(i), :], recv2[...])
        normed = norm_rows(home, gain(4)).astype(BF16)
        inner = gelu(dot_nn(normed, hh[...])).astype(BF16)
        out_ref[:, tile_rows(i)] = dot_nt(ho[...], inner)
        return carry

    lax.fori_loop(0, TILES, head, 0)
    wait_sent(1, send2, recv2)


def body(
    features, hilbert_rank, point_mask, norm_gains, w_qkv, w_out, w_up, w_down, head_hidden, head_out
):
    vmem = pl.BlockSpec(memory_space=pltpu.VMEM)
    away = pl.BlockSpec(memory_space=pl.ANY)
    rows = pltpu.VMEM((ROWS, WIDTH), BF16)
    slots = pltpu.VMEM((SLOTS, WIDTH), BF16)
    return pl.pallas_call(
        kernel,
        out_shape=jax.ShapeDtypeStruct((OUTS, ROWS), F32),
        in_specs=[vmem] * 4 + [away] * 6,
        out_specs=vmem,
        scratch_shapes=[
            rows,
            pltpu.VMEM((2, WIDTH, 3 * WIDTH), BF16),
            pltpu.VMEM((2, WIDTH, WIDTH), BF16),
            pltpu.VMEM((2, WIDTH, FF), BF16),
            pltpu.VMEM((2, FF, WIDTH), BF16),
            pltpu.VMEM((WIDTH, WIDTH), BF16),
            rows,
            pltpu.VMEM((ROWS, 1), F32),
            pltpu.VMEM((4, ROWS, WIDTH), BF16),
            pltpu.VMEM((4, ROWS, WIDTH), BF16),
            pltpu.VMEM((2, ROWS, WIDTH), BF16),
            rows,
            rows,
            pltpu.VMEM((1, ROWS), F32),
            pltpu.VMEM((PEERS, HALF), F32),
            pltpu.VMEM((PEERS, HALF), F32),
            pltpu.VMEM((ROWS, SLOTS), BF16),
            slots,
            slots,
            slots,
            slots,
            pltpu.SemaphoreType.DMA((6,)),
            pltpu.SemaphoreType.DMA((3,)),
            pltpu.SemaphoreType.DMA((3,)),
            pltpu.SemaphoreType.REGULAR,
        ],
        compiler_params=pltpu.CompilerParams(
            collective_id=0, has_side_effects=True, vmem_limit_bytes=56 * 2**20
        ),
    )(
        hilbert_rank[None, :], point_mask[None, :], norm_gains, head_out.T, features, w_qkv, w_out, w_up,
        w_down, head_hidden,
    ).T


def solution(mesh):
    spread = P(("rep", "pts"))
    in_specs = (P(("rep", "pts"), None), spread, spread) + (P(),) * 7
    return jax.shard_map(
        body, mesh=mesh, in_specs=in_specs, out_specs=P(("rep", "pts"), None), check_vma=False
    )
```

```python
import math

import jax
import jax.numpy as jnp
from jax import lax
from jax.experimental import pallas as pl
from jax.experimental.pallas import tpu as pltpu
from jax.sharding import PartitionSpec as P

NY, NX, NZ = 4, 4, 8
PEERS = NY * NX * NZ
ROOM = 16
ROWS = 1024
SLOTS = PEERS * ROOM
WIDTH = 256
HALF = 128
QUART = 64
DEPTH = 16
FF = 1024
OUTS = 4
TILE = 256
STEP = TILE // ROOM
TILES = ROWS // TILE
EARLY = 5
EPS = 1e-05
LOG2E = math.log2(math.e)
F32 = jnp.float32
BF16 = jnp.bfloat16
MESH = pl.DeviceIdType.MESH


def dot_nn(a, b):
    return lax.dot_general(a, b, (((1,), (0,)), ((), ())), preferred_element_type=F32)


def dot_nt(a, b):
    return lax.dot_general(a, b, (((1,), (1,)), ((), ())), preferred_element_type=F32)


def dot_tn(a, b):
    return lax.dot_general(a, b, (((0,), (0,)), ((), ())), preferred_element_type=F32)


def iota(shape, dim):
    return lax.broadcasted_iota(jnp.int32, shape, dim)


def ones_where(test):
    return jnp.where(test, 1.0, 0.0)


def norm_rows(values, gain):
    center = values - jnp.mean(values, axis=-1, keepdims=True)
    spread = jnp.mean(center * center, axis=-1, keepdims=True)
    return center * lax.rsqrt(spread + EPS) * gain


def gelu(x):
    size = jnp.abs(x)
    t = 1.0 / (1.0 + (0.3275911 / math.sqrt(2.0)) * size)
    poly = t * (
        0.5 * 0.254829592
        + t
        * (
            -0.5 * 0.284496736
            + t * (0.5 * 1.421413741 + t * (-0.5 * 1.453152027 + t * (0.5 * 1.061405429)))
        )
    )
    tail = poly * jnp.exp2(x * x * (-0.5 * LOG2E))
    return jnp.maximum(x, 0.0) - size * tail


def tile_rows(i, size=TILE):
    return pl.ds(pl.multiple_of(i * size, size), size)


def to_column(row):
    return jnp.transpose(jnp.broadcast_to(row, (HALF, row.shape[1])))[:, 0:1]


def starts_of(counts):
    below = ones_where(iota((PEERS, PEERS), 1) < iota((PEERS, PEERS), 0)).astype(BF16)
    wide = jnp.broadcast_to(counts, (PEERS, HALF)).astype(BF16)
    return dot_nn(below, wide)[:, 0:1]


def slots_of(counts, starts):
    place = iota((1, ROWS), 1).astype(F32)
    block = jnp.sum(ones_where(starts + counts <= place), axis=0, keepdims=True)
    begin = jnp.max(jnp.where(starts <= place, starts, 0.0), axis=0, keepdims=True)
    return block, place - begin


def project(x_ref, keep_ref, any_valid, gain, wqkv, q_ref, k_ref, v_ref):
    scale = jnp.where(any_valid > 0.0, 0.25 * LOG2E, 0.0)
    first_lane = iota((1, HALF), 1) == 0
    flag = jnp.broadcast_to(ones_where(first_lane), (TILE, HALF)).astype(BF16)

    def chunk(i, carry):
        rows = tile_rows(i)
        normed = norm_rows(x_ref[rows, :].astype(F32), gain).astype(BF16)
        qkv = dot_nn(normed, wqkv[...]).astype(BF16)
        drop = jnp.where(jnp.logical_and(any_valid > 0.0, keep_ref[rows, :] < 0.5), -1e30, 0.0)
        bias = jnp.where(first_lane, drop, 0.0).astype(BF16)
        for g in range(4):
            q = qkv[:, QUART * g : QUART * (g + 1)].astype(F32) * scale
            high = q.astype(BF16)
            low = (q - high.astype(F32)).astype(BF16)
            k = qkv[:, WIDTH + QUART * g : WIDTH + QUART * (g + 1)]
            q_ref[g, rows, 0:HALF] = jnp.concatenate([high, low], axis=1)
            q_ref[g, rows, HALF:WIDTH] = flag
            k_ref[g, rows, 0:HALF] = jnp.concatenate([k, k], axis=1)
            k_ref[g, rows, HALF:WIDTH] = bias
        for g in range(2):
            v_ref[g, rows, 0:HALF] = qkv[:, 2 * WIDTH + HALF * g : 2 * WIDTH + HALF * (g + 1)]
            v_ref[g, rows, HALF:WIDTH] = jnp.ones((TILE, HALF), BF16)
        return carry

    lax.fori_loop(0, TILES, chunk, 0, unroll=2)


def attend(rows, q_ref, k_ref, v_ref, between=()):
    lane = iota((1, WIDTH), 1)
    steps = list(between)

    def scores_of(n):
        quad, inner = n // 4, n % 4
        mine = jnp.logical_or(
            jnp.logical_and(lane < HALF, (lane % QUART) // DEPTH == inner), lane == HALF
        )
        query = q_ref[quad, rows, :] * ones_where(mine).astype(BF16)
        return dot_nt(query, k_ref[quad])

    both = []
    scores = scores_of(0)
    for g in range(2):
        total = None
        for h in range(8):
            n = 8 * g + h
            following = scores_of(n + 1) if n < 15 else None
            top = jnp.max(scores, axis=-1, keepdims=True)
            expo = jnp.exp2(scores - top).astype(BF16)
            picked = ones_where((lane % HALF) // DEPTH == h).astype(BF16)
            part = dot_nn(expo, v_ref[g] * picked)
            total = part if total is None else total + part
            scores = following
            if steps:
                steps.pop(0)()
        both.append((total[:, 0:HALF] / total[:, HALF:WIDTH]).astype(BF16))
    return jnp.concatenate(both, axis=1)


def finish_steps(x_ref, m_ref, y_ref, rows, gain, wo, wu, wd):
    held = {}

    def begin():
        held["sum"] = x_ref[rows, :].astype(F32) + dot_nn(m_ref[rows, :], wo[...])
        held["normed"] = norm_rows(held["sum"], gain).astype(BF16)

    def part(c):
        def step():
            hidden = gelu(dot_nn(held["normed"], wu[:, WIDTH * c : WIDTH * (c + 1)])).astype(BF16)
            held["sum"] = held["sum"] + dot_nn(hidden, wd[WIDTH * c : WIDTH * (c + 1), :])

        return step

    def end():
        y_ref[rows, :] = held["sum"].astype(BF16)

    return [begin] + [part(c) for c in range(FF // WIDTH)] + [end]


def kernel(
    rank_ref, mask_ref, gains_ref, ho, x_hbm, wqkv_hbm, wo_hbm, wu_hbm, wd_hbm, hh_hbm, out_ref,
    x_ref, wqkv, wo, wu, wd, hh, xs_ref, keep_ref, q_ref, k_ref, v_ref, m_ref, y_ref,
    slot_ref, codes, got_codes, pick_ref, send1, recv1, send2, recv2, load_sem, send_sem, recv_sem,
    go_sem,
):
    me = lax.axis_index("pts")
    rep = lax.axis_index("rep")
    my_y, my_x, my_z = me // (NX * NZ), (me // NZ) % NX, me % NZ

    def peer_of(k, sign):
        c, e = k // (NX * NY), NX * NY - 1 - k % (NX * NY)
        dz = NZ // 2 + c // 2 - (c % 2) * (1 + 2 * (c // 2))
        y = (my_y + NY + sign * (e // NX)) % NY
        x = (my_x + NX + sign * (e % NX)) % NX
        z = (my_z + NZ + sign * dz) % NZ
        return (y * NX + x) * NZ + z

    loads = [
        pltpu.make_async_copy(source, target, load_sem.at[n])
        for n, (source, target) in enumerate(
            (
                (x_hbm, x_ref), (wqkv_hbm, wqkv), (wo_hbm, wo), (wu_hbm, wu), (wd_hbm, wd),
                (hh_hbm, hh),
            )
        )
    ]
    for load in loads:
        load.start()

    barrier = pltpu.get_barrier_semaphore()

    def greet(k, carry):
        pl.semaphore_signal(barrier, inc=1, device_id={"pts": peer_of(k, 1)}, device_id_type=MESH)
        return carry

    lax.fori_loop(0, PEERS - 1, greet, 0)
    partner = {"rep": 1 - rep}
    pl.semaphore_signal(barrier, inc=1, device_id=partner, device_id_type=MESH)

    def gain(n):
        return gains_ref[n : n + 1, :].astype(F32)

    def send_blocks(which, source, target, low, high, sign):
        def one(k, carry):
            rows = pl.ds(pl.multiple_of(k * ROOM, ROOM), ROOM)
            pltpu.make_async_remote_copy(
                src_ref=source.at[rows], dst_ref=target.at[rows],
                send_sem=send_sem.at[which], recv_sem=recv_sem.at[which],
                device_id={"pts": peer_of(k, sign)}, device_id_type=MESH,
            ).start()
            return carry

        lax.fori_loop(low, high, one, 0)

    def keep_own(which, source, target):
        rows = pl.ds(SLOTS - ROOM, ROOM)
        pltpu.make_async_copy(source.at[rows], target.at[rows], recv_sem.at[which]).start()

    def wait_sent(which, source, target):
        rows = pl.ds(0, SLOTS - ROOM)
        pltpu.make_async_copy(source.at[rows], target.at[rows], send_sem.at[which]).wait()

    def wait_received(which, source, target):
        pltpu.make_async_copy(source, target, recv_sem.at[which]).wait()

    target = rank_ref[...] // ROWS
    step_z = (target % NZ - my_z + NZ) % NZ
    step_x = (target // NZ % NX - my_x + NX) % NX
    step_y = (target // (NX * NZ) - my_y + NY) % NY
    order = jnp.where(step_z < NZ // 2, NZ - 1 - 2 * step_z, 2 * step_z - NZ)
    block = (order * (NX * NY) + NX * NY - 1 - (step_y * NX + step_x)).astype(F32)
    valid = ones_where(mask_ref[...] > 0)
    hot = ones_where(iota((PEERS, 1), 0).astype(F32) == block)
    counts = jnp.sum(hot, axis=1, keepdims=True)
    starts = starts_of(counts)
    earlier = ones_where(iota((ROWS, ROWS), 0) < iota((ROWS, ROWS), 1)).astype(BF16)
    before = dot_nn(hot.astype(BF16), earlier)
    within = jnp.sum(hot * before, axis=0, keepdims=True)
    place = within + jnp.sum(hot * starts, axis=0, keepdims=True)
    home_slot = to_column(block * ROOM + within)
    marks = jnp.where(iota((HALF, 1), 0).astype(F32) == within, 1.0 + valid, 0.0)
    codes[...] = dot_nt(hot.astype(BF16), marks.astype(BF16))
    sorted_block, sorted_within = slots_of(counts, starts)
    slot_ref[...] = sorted_block * ROOM + sorted_within
    y_ref[...] = jnp.zeros((ROWS, WIDTH), BF16)
    loads[0].wait()

    def sort(i, carry):
        want = (iota((TILE, 1), 0) + i * TILE).astype(F32)
        pick = ones_where(want == place)
        xs_ref[tile_rows(i), :] = dot_nn(pick.astype(BF16), x_ref[...]).astype(BF16)
        keep_ref[tile_rows(i), :] = jnp.sum(pick * valid, axis=1, keepdims=True)
        return carry

    lax.fori_loop(0, TILES, sort, 0)
    for load in loads[1:]:
        load.wait()

    def pack(i, send_ref):
        slot = (iota((TILE, 1), 0) + i * TILE).astype(F32)
        pick = ones_where(slot == slot_ref[...]).astype(BF16)
        send_ref[tile_rows(i), :] = dot_nn(pick, y_ref[...]).astype(BF16)

    def send_step(i, send_ref, recv_ref, which, sign):
        send_blocks(which, send_ref, recv_ref, STEP * i, STEP * (i + 1), sign)

    def run_block(index, any_valid, send_ref, recv_ref, which, sign):
        weights = (wo.at[index], wu.at[index], wd.at[index])
        project(
            xs_ref, keep_ref, any_valid, gain(2 * index), wqkv.at[index], q_ref, k_ref, v_ref
        )

        def steps(i):
            rest = finish_steps(
                xs_ref, m_ref, y_ref, tile_rows(i), gain(2 * index + 1), *weights
            )
            return rest + [lambda: pack(i, send_ref)]

        m_ref[tile_rows(0), :] = attend(tile_rows(0), q_ref, k_ref, v_ref)
        if index == 0:
            pl.semaphore_wait(barrier, PEERS)

            def one(k, carry):
                row = pl.ds(k, 1)
                pltpu.make_async_remote_copy(
                    src_ref=codes.at[row], dst_ref=got_codes.at[row],
                    send_sem=send_sem.at[2], recv_sem=recv_sem.at[2],
                    device_id={"pts": peer_of(k, 1)}, device_id_type=MESH,
                ).start()
                return carry

            lax.fori_loop(0, PEERS - 1, one, 0)
            row = pl.ds(PEERS - 1, 1)
            pltpu.make_async_copy(codes.at[row], got_codes.at[row], recv_sem.at[2]).start()

        def later(i, carry):
            between = steps(i - 1) + [lambda: send_step(i - 1, send_ref, recv_ref, which, sign)]
            m_ref[tile_rows(i), :] = attend(tile_rows(i), q_ref, k_ref, v_ref, between)
            return carry

        lax.fori_loop(1, TILES, later, 0)
        for step in steps(TILES - 1):
            step()

    chunks = SLOTS // TILE

    def send_rest(send_ref, recv_ref, which, sign, sent):
        send_step(TILES - 1, send_ref, recv_ref, which, sign)
        for i in range(TILES, chunks):
            pack(i, send_ref)
            if i < sent:
                high = min(STEP * (i + 1), PEERS - 1)
                send_blocks(which, send_ref, recv_ref, STEP * i, high, sign)

    run_block(0, jnp.max(valid, axis=(0, 1), keepdims=True), send1, recv1, 0, 1)

    @pl.when(rep == 0)
    def _():
        send_rest(send1, recv1, 0, 1, chunks)

    @pl.when(rep == 1)
    def _():
        send_rest(send1, recv1, 0, 1, EARLY)

    keep_own(0, send1, recv1)

    pltpu.make_async_copy(codes, got_codes, recv_sem.at[2]).wait()
    wait_codes = pl.ds(0, PEERS - 1)
    pltpu.make_async_copy(codes.at[wait_codes], got_codes.at[wait_codes], send_sem.at[2]).wait()
    code = got_codes[...]
    counts2 = jnp.sum(ones_where(code > 0.5), axis=1, keepdims=True)
    starts2 = starts_of(counts2)
    block2, within2 = slots_of(counts2, starts2)
    slot2 = block2 * ROOM + within2
    slot_ref[...] = slot2
    hot2 = ones_where(iota((PEERS, 1), 0).astype(F32) == block2).astype(BF16)
    marks2 = dot_tn(code.astype(BF16), hot2)
    mark = jnp.where(iota((HALF, 1), 0).astype(F32) == within2, marks2, 0.0)
    valid2 = ones_where(jnp.sum(mark, axis=0, keepdims=True) > 1.5)
    keep_ref[...] = to_column(valid2)
    slot_column = to_column(slot2)
    lanes = iota((1, SLOTS), 1).astype(F32)
    pick_ref[...] = ones_where(slot_column == lanes).astype(BF16)

    @pl.when(rep == 0)
    def _():
        wait_sent(0, send1, recv1)
        pl.semaphore_signal(go_sem, inc=1, device_id=partner, device_id_type=MESH)

    @pl.when(rep == 1)
    def _():
        pl.semaphore_wait(go_sem, 1)
        send_blocks(0, send1, recv1, STEP * EARLY, PEERS - 1, 1)

    wait_received(0, send1, recv1)

    def unpack(i, carry):
        xs_ref[tile_rows(i), :] = dot_nn(pick_ref[tile_rows(i), :], recv1[...]).astype(BF16)
        return carry

    lax.fori_loop(0, TILES, unpack, 0, unroll=True)
    run_block(1, jnp.max(valid2, axis=(0, 1), keepdims=True), send2, recv2, 1, -1)
    send_rest(send2, recv2, 1, -1, chunks)
    keep_own(1, send2, recv2)

    pick_ref[...] = ones_where(home_slot == lanes).astype(BF16)

    @pl.when(rep == 1)
    def _():
        wait_sent(0, send1, recv1)

    wait_received(1, send2, recv2)

    def head(i, carry):
        home = dot_nn(pick_ref[tile_rows(i), :], recv2[...])
        normed = norm_rows(home, gain(4)).astype(BF16)
        inner = gelu(dot_nn(normed, hh[...])).astype(BF16)
        out_ref[:, tile_rows(i)] = dot_nt(ho[...], inner)
        return carry

    lax.fori_loop(0, TILES, head, 0, unroll=True)
    wait_sent(1, send2, recv2)


def body(
    features, hilbert_rank, point_mask, norm_gains, w_qkv, w_out, w_up, w_down, head_hidden, head_out
):
    vmem = pl.BlockSpec(memory_space=pltpu.VMEM)
    away = pl.BlockSpec(memory_space=pl.ANY)
    rows = pltpu.VMEM((ROWS, WIDTH), BF16)
    slots = pltpu.VMEM((SLOTS, WIDTH), BF16)
    return pl.pallas_call(
        kernel,
        out_shape=jax.ShapeDtypeStruct((OUTS, ROWS), F32),
        in_specs=[vmem] * 4 + [away] * 6,
        out_specs=vmem,
        scratch_shapes=[
            rows,
            pltpu.VMEM((2, WIDTH, 3 * WIDTH), BF16),
            pltpu.VMEM((2, WIDTH, WIDTH), BF16),
            pltpu.VMEM((2, WIDTH, FF), BF16),
            pltpu.VMEM((2, FF, WIDTH), BF16),
            pltpu.VMEM((WIDTH, WIDTH), BF16),
            rows,
            pltpu.VMEM((ROWS, 1), F32),
            pltpu.VMEM((4, ROWS, WIDTH), BF16),
            pltpu.VMEM((4, ROWS, WIDTH), BF16),
            pltpu.VMEM((2, ROWS, WIDTH), BF16),
            rows,
            rows,
            pltpu.VMEM((1, ROWS), F32),
            pltpu.VMEM((PEERS, HALF), F32),
            pltpu.VMEM((PEERS, HALF), F32),
            pltpu.VMEM((ROWS, SLOTS), BF16),
            slots,
            slots,
            slots,
            slots,
            pltpu.SemaphoreType.DMA((6,)),
            pltpu.SemaphoreType.DMA((3,)),
            pltpu.SemaphoreType.DMA((3,)),
            pltpu.SemaphoreType.REGULAR,
        ],
        compiler_params=pltpu.CompilerParams(
            collective_id=0, has_side_effects=True, vmem_limit_bytes=56 * 2**20
        ),
    )(
        hilbert_rank[None, :], point_mask[None, :], norm_gains, head_out.T, features, w_qkv, w_out, w_up,
        w_down, head_hidden,
    ).T


def solution(mesh):
    spread = P(("rep", "pts"))
    in_specs = (P(("rep", "pts"), None), spread, spread) + (P(),) * 7
    return jax.shard_map(
        body, mesh=mesh, in_specs=in_specs, out_specs=P(("rep", "pts"), None), check_vma=False
    )
```

```python
import math

import jax
import jax.numpy as jnp
from jax import lax
from jax.experimental import pallas as pl
from jax.experimental.pallas import tpu as pltpu
from jax.sharding import PartitionSpec as P

NY, NX, NZ = 4, 4, 8
PEERS = NY * NX * NZ
ROOM = 16
ROWS = 1024
SLOTS = PEERS * ROOM
WIDTH = 256
HALF = 128
QUART = 64
DEPTH = 16
FF = 1024
OUTS = 4
TILE = 256
STEP = TILE // ROOM
TILES = ROWS // TILE
EARLY = 5
EPS = 1e-05
LOG2E = math.log2(math.e)
F32 = jnp.float32
BF16 = jnp.bfloat16
MESH = pl.DeviceIdType.MESH


def dot_nn(a, b):
    return lax.dot_general(a, b, (((1,), (0,)), ((), ())), preferred_element_type=F32)


def dot_nt(a, b):
    return lax.dot_general(a, b, (((1,), (1,)), ((), ())), preferred_element_type=F32)


def dot_tn(a, b):
    return lax.dot_general(a, b, (((0,), (0,)), ((), ())), preferred_element_type=F32)


def iota(shape, dim):
    return lax.broadcasted_iota(jnp.int32, shape, dim)


def ones_where(test):
    return jnp.where(test, 1.0, 0.0)


def norm_rows(values, gain):
    center = values - jnp.mean(values, axis=-1, keepdims=True)
    spread = jnp.mean(center * center, axis=-1, keepdims=True)
    return center * lax.rsqrt(spread + EPS) * gain


def gelu(x):
    size = jnp.abs(x)
    t = 1.0 / (1.0 + (0.3275911 / math.sqrt(2.0)) * size)
    poly = t * (
        0.5 * 0.254829592
        + t
        * (
            -0.5 * 0.284496736
            + t * (0.5 * 1.421413741 + t * (-0.5 * 1.453152027 + t * (0.5 * 1.061405429)))
        )
    )
    tail = poly * jnp.exp2(x * x * (-0.5 * LOG2E))
    return jnp.maximum(x, 0.0) - size * tail


def tile_rows(i, size=TILE):
    return pl.ds(pl.multiple_of(i * size, size), size)


def to_column(row):
    return jnp.transpose(jnp.broadcast_to(row, (HALF, row.shape[1])))[:, 0:1]


def starts_of(counts):
    below = ones_where(iota((PEERS, PEERS), 1) < iota((PEERS, PEERS), 0)).astype(BF16)
    wide = jnp.broadcast_to(counts, (PEERS, HALF)).astype(BF16)
    return dot_nn(below, wide)[:, 0:1]


def slots_of(counts, starts):
    place = iota((1, ROWS), 1).astype(F32)
    block = jnp.sum(ones_where(starts + counts <= place), axis=0, keepdims=True)
    begin = jnp.max(jnp.where(starts <= place, starts, 0.0), axis=0, keepdims=True)
    return block, place - begin


def project(x_ref, keep_ref, any_valid, gain, wqkv, q_ref, k_ref, v_ref):
    scale = jnp.where(any_valid > 0.0, 0.25 * LOG2E, 0.0)
    first_lane = iota((1, HALF), 1) == 0
    flag = jnp.broadcast_to(ones_where(first_lane), (TILE, HALF)).astype(BF16)

    def chunk(i, carry):
        rows = tile_rows(i)
        normed = norm_rows(x_ref[rows, :].astype(F32), gain).astype(BF16)
        qkv = dot_nn(normed, wqkv[...]).astype(BF16)
        drop = jnp.where(jnp.logical_and(any_valid > 0.0, keep_ref[rows, :] < 0.5), -1e30, 0.0)
        bias = jnp.where(first_lane, drop, 0.0).astype(BF16)
        for g in range(4):
            q = qkv[:, QUART * g : QUART * (g + 1)].astype(F32) * scale
            high = q.astype(BF16)
            low = (q - high.astype(F32)).astype(BF16)
            k = qkv[:, WIDTH + QUART * g : WIDTH + QUART * (g + 1)]
            q_ref[g, rows, 0:HALF] = jnp.concatenate([high, low], axis=1)
            q_ref[g, rows, HALF:WIDTH] = flag
            k_ref[g, rows, 0:HALF] = jnp.concatenate([k, k], axis=1)
            k_ref[g, rows, HALF:WIDTH] = bias
        for g in range(2):
            v_ref[g, rows, 0:HALF] = qkv[:, 2 * WIDTH + HALF * g : 2 * WIDTH + HALF * (g + 1)]
            v_ref[g, rows, HALF:WIDTH] = jnp.ones((TILE, HALF), BF16)
        return carry

    lax.fori_loop(0, TILES, chunk, 0, unroll=2)


def attend(rows, q_ref, k_ref, v_ref, between=()):
    lane = iota((1, WIDTH), 1)
    steps = list(between)

    def scores_of(n):
        quad, inner = n // 4, n % 4
        mine = jnp.logical_or(
            jnp.logical_and(lane < HALF, (lane % QUART) // DEPTH == inner), lane == HALF
        )
        query = q_ref[quad, rows, :] * ones_where(mine).astype(BF16)
        return dot_nt(query, k_ref[quad])

    both = []
    scores = scores_of(0)
    for g in range(2):
        total = None
        for h in range(8):
            n = 8 * g + h
            following = scores_of(n + 1) if n < 15 else None
            top = jnp.max(scores, axis=-1, keepdims=True)
            expo = jnp.exp2(scores - top).astype(BF16)
            picked = ones_where((lane % HALF) // DEPTH == h).astype(BF16)
            part = dot_nn(expo, v_ref[g] * picked)
            total = part if total is None else total + part
            scores = following
            if steps:
                steps.pop(0)()
        both.append((total[:, 0:HALF] / total[:, HALF:WIDTH]).astype(BF16))
    return jnp.concatenate(both, axis=1)


def finish_steps(x_ref, m_ref, y_ref, rows, gain, wo, wu, wd):
    held = {}

    def begin():
        held["sum"] = x_ref[rows, :].astype(F32) + dot_nn(m_ref[rows, :], wo[...])
        held["normed"] = norm_rows(held["sum"], gain).astype(BF16)

    def part(c):
        def step():
            hidden = gelu(dot_nn(held["normed"], wu[:, WIDTH * c : WIDTH * (c + 1)])).astype(BF16)
            held["sum"] = held["sum"] + dot_nn(hidden, wd[WIDTH * c : WIDTH * (c + 1), :])

        return step

    def end():
        y_ref[rows, :] = held["sum"].astype(BF16)

    return [begin] + [part(c) for c in range(FF // WIDTH)] + [end]


def kernel(
    rank_ref, mask_ref, gains_ref, ho, x_hbm, wqkv_hbm, wo_hbm, wu_hbm, wd_hbm, hh_hbm, out_ref,
    x_ref, wqkv, wo, wu, wd, hh, xs_ref, keep_ref, q_ref, k_ref, v_ref, m_ref, y_ref,
    slot_ref, codes, got_codes, pick_ref, send1, recv1, send2, recv2, load_sem, send_sem, recv_sem,
    go_sem,
):
    me = lax.axis_index("pts")
    rep = lax.axis_index("rep")
    my_y, my_x, my_z = me // (NX * NZ), (me // NZ) % NX, me % NZ

    def over_chunk(c, sign, act, last=False):
        dz = NZ // 2 + c // 2 - (c % 2) * (1 + 2 * (c // 2))
        zs = [lax.rem(my_z + way * sign * dz + NZ, NZ) for way in (1, -1)]
        xs = [lax.rem(my_x + sign * (NX - 1 - j) + NX, NX) for j in range(NX)]

        def line(i, carry):
            y = lax.rem(my_y + sign * (NY - 1 - i) + NY, NY)
            for j in range(NX):
                if not (last and carry is None and j == NX - 1):
                    act((c * NY + i) * NX + j, (y * NX + xs[j]) * NZ + zs[j % 2])
            return carry

        lax.fori_loop(0, NY - 1 if last else NY, line, 0)
        if last:
            line(NY - 1, None)

    loads = [
        pltpu.make_async_copy(source, target, load_sem.at[n])
        for n, (source, target) in enumerate(
            (
                (x_hbm, x_ref), (wqkv_hbm, wqkv), (wo_hbm, wo), (wu_hbm, wu), (wd_hbm, wd),
                (hh_hbm, hh),
            )
        )
    ]
    for load in loads:
        load.start()

    barrier = pltpu.get_barrier_semaphore()

    def greet(k, carry):
        peer = lax.rem(me + k, PEERS)
        pl.semaphore_signal(barrier, inc=1, device_id={"pts": peer}, device_id_type=MESH)
        return carry

    lax.fori_loop(1, PEERS, greet, 0)
    partner = {"rep": 1 - rep}
    pl.semaphore_signal(barrier, inc=1, device_id=partner, device_id_type=MESH)

    def gain(n):
        return gains_ref[n : n + 1, :].astype(F32)

    def send_chunk(which, source, target, c, sign, last=False):
        def one(k, peer):
            rows = pl.ds(pl.multiple_of(k * ROOM, ROOM), ROOM)
            pltpu.make_async_remote_copy(
                src_ref=source.at[rows], dst_ref=target.at[rows],
                send_sem=send_sem.at[which], recv_sem=recv_sem.at[which],
                device_id={"pts": peer}, device_id_type=MESH,
            ).start()

        over_chunk(c, sign, one, last)

    def keep_own(which, source, target):
        rows = pl.ds(SLOTS - ROOM, ROOM)
        pltpu.make_async_copy(source.at[rows], target.at[rows], recv_sem.at[which]).start()

    def wait_sent(which, source, target):
        rows = pl.ds(0, SLOTS - ROOM)
        pltpu.make_async_copy(source.at[rows], target.at[rows], send_sem.at[which]).wait()

    def wait_received(which, source, target):
        pltpu.make_async_copy(source, target, recv_sem.at[which]).wait()

    target = rank_ref[...] // ROWS
    step_z = (target % NZ - my_z + NZ) % NZ
    step_x = (target // NZ % NX - my_x + NX) % NX
    step_y = (target // (NX * NZ) - my_y + NY) % NY
    step_z = jnp.where(step_x % 2 == (NX - 1) % 2, step_z, (NZ - step_z) % NZ)
    order = jnp.where(step_z < NZ // 2, NZ - 1 - 2 * step_z, 2 * step_z - NZ)
    block = (order * (NX * NY) + NX * NY - 1 - (step_y * NX + step_x)).astype(F32)
    valid = ones_where(mask_ref[...] > 0)
    hot = ones_where(iota((PEERS, 1), 0).astype(F32) == block)
    counts = jnp.sum(hot, axis=1, keepdims=True)
    starts = starts_of(counts)
    earlier = ones_where(iota((ROWS, ROWS), 0) < iota((ROWS, ROWS), 1)).astype(BF16)
    before = dot_nn(hot.astype(BF16), earlier)
    within = jnp.sum(hot * before, axis=0, keepdims=True)
    place = within + jnp.sum(hot * starts, axis=0, keepdims=True)
    home_slot = to_column(block * ROOM + within)
    marks = jnp.where(iota((HALF, 1), 0).astype(F32) == within, 1.0 + valid, 0.0)
    codes[...] = dot_nt(hot.astype(BF16), marks.astype(BF16))
    sorted_block, sorted_within = slots_of(counts, starts)
    slot_ref[...] = sorted_block * ROOM + sorted_within
    y_ref[...] = jnp.zeros((ROWS, WIDTH), BF16)
    loads[0].wait()

    def sort(i, carry):
        want = (iota((TILE, 1), 0) + i * TILE).astype(F32)
        pick = ones_where(want == place)
        xs_ref[tile_rows(i), :] = dot_nn(pick.astype(BF16), x_ref[...]).astype(BF16)
        keep_ref[tile_rows(i), :] = jnp.sum(pick * valid, axis=1, keepdims=True)
        return carry

    lax.fori_loop(0, TILES, sort, 0)
    for load in loads[1:]:
        load.wait()

    def pack(i, send_ref):
        slot = (iota((TILE, 1), 0) + i * TILE).astype(F32)
        pick = ones_where(slot == slot_ref[...]).astype(BF16)
        send_ref[tile_rows(i), :] = dot_nn(pick, y_ref[...]).astype(BF16)

    def run_block(index, any_valid, send_ref, recv_ref, which, sign):
        weights = (wo.at[index], wu.at[index], wd.at[index])
        project(
            xs_ref, keep_ref, any_valid, gain(2 * index), wqkv.at[index], q_ref, k_ref, v_ref
        )

        def steps(i):
            rest = finish_steps(
                xs_ref, m_ref, y_ref, tile_rows(i), gain(2 * index + 1), *weights
            )
            return rest + [lambda: pack(i, send_ref)]

        m_ref[tile_rows(0), :] = attend(tile_rows(0), q_ref, k_ref, v_ref)
        if index == 0:
            pl.semaphore_wait(barrier, PEERS)

            def one(k, peer):
                row = pl.ds(k, 1)
                pltpu.make_async_remote_copy(
                    src_ref=codes.at[row], dst_ref=got_codes.at[row],
                    send_sem=send_sem.at[2], recv_sem=recv_sem.at[2],
                    device_id={"pts": peer}, device_id_type=MESH,
                ).start()

            def codes_chunk(c, carry):
                over_chunk(c, 1, one)
                return carry

            lax.fori_loop(0, NZ - 1, codes_chunk, 0)
            over_chunk(NZ - 1, 1, one, True)
            row = pl.ds(PEERS - 1, 1)
            pltpu.make_async_copy(codes.at[row], got_codes.at[row], recv_sem.at[2]).start()

        def later(i, carry):
            between = steps(i - 1) + [lambda: send_chunk(which, send_ref, recv_ref, i - 1, sign)]
            m_ref[tile_rows(i), :] = attend(tile_rows(i), q_ref, k_ref, v_ref, between)
            return carry

        lax.fori_loop(1, TILES, later, 0)
        for step in steps(TILES - 1):
            step()

    chunks = SLOTS // TILE

    def send_rest(send_ref, recv_ref, which, sign, sent):
        send_chunk(which, send_ref, recv_ref, TILES - 1, sign)
        for i in range(TILES, chunks):
            pack(i, send_ref)
            if i < sent:
                send_chunk(which, send_ref, recv_ref, i, sign, i == chunks - 1)

    run_block(0, jnp.max(valid, axis=(0, 1), keepdims=True), send1, recv1, 0, 1)

    @pl.when(rep == 0)
    def _():
        send_rest(send1, recv1, 0, 1, chunks)

    @pl.when(rep == 1)
    def _():
        send_rest(send1, recv1, 0, 1, EARLY)

    keep_own(0, send1, recv1)

    pltpu.make_async_copy(codes, got_codes, recv_sem.at[2]).wait()
    wait_codes = pl.ds(0, PEERS - 1)
    pltpu.make_async_copy(codes.at[wait_codes], got_codes.at[wait_codes], send_sem.at[2]).wait()
    code = got_codes[...]
    counts2 = jnp.sum(ones_where(code > 0.5), axis=1, keepdims=True)
    starts2 = starts_of(counts2)
    block2, within2 = slots_of(counts2, starts2)
    slot2 = block2 * ROOM + within2
    slot_ref[...] = slot2
    hot2 = ones_where(iota((PEERS, 1), 0).astype(F32) == block2).astype(BF16)
    marks2 = dot_tn(code.astype(BF16), hot2)
    mark = jnp.where(iota((HALF, 1), 0).astype(F32) == within2, marks2, 0.0)
    valid2 = ones_where(jnp.sum(mark, axis=0, keepdims=True) > 1.5)
    keep_ref[...] = to_column(valid2)
    slot_column = to_column(slot2)
    lanes = iota((1, SLOTS), 1).astype(F32)
    pick_ref[...] = ones_where(slot_column == lanes).astype(BF16)

    @pl.when(rep == 0)
    def _():
        wait_sent(0, send1, recv1)
        pl.semaphore_signal(go_sem, inc=1, device_id=partner, device_id_type=MESH)

    @pl.when(rep == 1)
    def _():
        pl.semaphore_wait(go_sem, 1)
        for i in range(EARLY, chunks):
            send_chunk(0, send1, recv1, i, 1, i == chunks - 1)

    wait_received(0, send1, recv1)

    def unpack(i, carry):
        xs_ref[tile_rows(i), :] = dot_nn(pick_ref[tile_rows(i), :], recv1[...]).astype(BF16)
        return carry

    lax.fori_loop(0, TILES, unpack, 0, unroll=True)
    run_block(1, jnp.max(valid2, axis=(0, 1), keepdims=True), send2, recv2, 1, -1)
    send_rest(send2, recv2, 1, -1, chunks)
    keep_own(1, send2, recv2)

    pick_ref[...] = ones_where(home_slot == lanes).astype(BF16)

    @pl.when(rep == 1)
    def _():
        wait_sent(0, send1, recv1)

    wait_received(1, send2, recv2)

    def head(i, carry):
        home = dot_nn(pick_ref[tile_rows(i), :], recv2[...])
        normed = norm_rows(home, gain(4)).astype(BF16)
        inner = gelu(dot_nn(normed, hh[...])).astype(BF16)
        out_ref[:, tile_rows(i)] = dot_nt(ho[...], inner)
        return carry

    lax.fori_loop(0, TILES, head, 0, unroll=True)
    wait_sent(1, send2, recv2)


def body(
    features, hilbert_rank, point_mask, norm_gains, w_qkv, w_out, w_up, w_down, head_hidden, head_out
):
    vmem = pl.BlockSpec(memory_space=pltpu.VMEM)
    away = pl.BlockSpec(memory_space=pl.ANY)
    rows = pltpu.VMEM((ROWS, WIDTH), BF16)
    slots = pltpu.VMEM((SLOTS, WIDTH), BF16)
    return pl.pallas_call(
        kernel,
        out_shape=jax.ShapeDtypeStruct((OUTS, ROWS), F32),
        in_specs=[vmem] * 4 + [away] * 6,
        out_specs=vmem,
        scratch_shapes=[
            rows,
            pltpu.VMEM((2, WIDTH, 3 * WIDTH), BF16),
            pltpu.VMEM((2, WIDTH, WIDTH), BF16),
            pltpu.VMEM((2, WIDTH, FF), BF16),
            pltpu.VMEM((2, FF, WIDTH), BF16),
            pltpu.VMEM((WIDTH, WIDTH), BF16),
            rows,
            pltpu.VMEM((ROWS, 1), F32),
            pltpu.VMEM((4, ROWS, WIDTH), BF16),
            pltpu.VMEM((4, ROWS, WIDTH), BF16),
            pltpu.VMEM((2, ROWS, WIDTH), BF16),
            rows,
            rows,
            pltpu.VMEM((1, ROWS), F32),
            pltpu.VMEM((PEERS, HALF), F32),
            pltpu.VMEM((PEERS, HALF), F32),
            pltpu.VMEM((ROWS, SLOTS), BF16),
            slots,
            slots,
            slots,
            slots,
            pltpu.SemaphoreType.DMA((6,)),
            pltpu.SemaphoreType.DMA((3,)),
            pltpu.SemaphoreType.DMA((3,)),
            pltpu.SemaphoreType.REGULAR,
        ],
        compiler_params=pltpu.CompilerParams(
            collective_id=0, has_side_effects=True, vmem_limit_bytes=56 * 2**20
        ),
    )(
        hilbert_rank[None, :], point_mask[None, :], norm_gains, head_out.T, features, w_qkv, w_out, w_up,
        w_down, head_hidden,
    ).T


def solution(mesh):
    spread = P(("rep", "pts"))
    in_specs = (P(("rep", "pts"), None), spread, spread) + (P(),) * 7
    return jax.shard_map(
        body, mesh=mesh, in_specs=in_specs, out_specs=P(("rep", "pts"), None), check_vma=False
    )
```
